32 devices in a mesh: pipe: 4 (over z), dp: 8 (over y, x, core).
Axes of the slice: x: 2, y: 2, z: 4, core: 2. Of those that a mesh axis runs over, the one named last changes fastest.
Arguments:
- section_inputs: bfloat16 [4096, 6144], P(('pipe', 'dp')), may hold values from -6 to 6
- out_grad: bfloat16 [1024, 6144], P('dp'), may hold values from -6 to 6
- up_weight: bfloat16 [512, 6144], P('pipe'), may hold values from -0.078125 to 0.078125
- down_weight: bfloat16 [512, 6144], P('pipe'), may hold values from -0.078125 to 0.078125
- momentum: bfloat16 [1024, 6144], P('pipe'), may hold values from -4 to 4
- worker_error: bfloat16 [1024, 49152], P('pipe', 'dp'), may hold values from -4 to 4
- server_error: float32 [1024, 6144], P('pipe', 'dp'), may hold values from -3 to 3
- owner_map: int32 [8], replicated, may hold values from 0 to 7, each once
Outputs:
- new_momentum: bfloat16 [1024, 6144], P('pipe')
- new_worker_error: bfloat16 [1024, 49152], P('pipe', 'dp')
- new_server_error: float32 [1024, 6144], P('pipe', 'dp')
The draws below stay inside these ranges and needn't reach their ends.
Inputs may be any that keep to these rules, and one draw needn't show every extreme that they name: owner_map names every worker exactly once.
All inputs are finite; a program needn't handle non-finite values. Where the reference program divides by a largest or mean magnitude, that divisor is 1e-20 or more.
Results may differ from the reference program's by a relative error of at most 0.0085.
Values may be sent and summed in bfloat16 or wider, within the bound.
A program may use at most 128 MiB of HBM per device.

```python
import jax
import jax.numpy as jnp
from jax import lax

D = 6144
FFW = 128
TOK_DEV = 128
PROWS = 256
CW = 768
N_PIPE = 4
N_DP = 8


def level_of(rng, dims, cuts, smallest, high):
    level = 1.0
    for position, shards_of in cuts:
        steps = jax.random.uniform(jax.random.fold_in(jax.random.fold_in(rng, 6), position), (shards_of,), jnp.float32, smallest / len(cuts), high / len(cuts))
        level = level * jnp.repeat(jnp.exp(steps), dims[position] // shards_of).reshape((-1,) + (1,) * (len(dims) - 1 - position))
    return level


def gaussian(rng, extent, deviation, reach, cuts=(), dtype=jnp.bfloat16):
    factor_of = level_of(rng, extent, cuts, -0.22, 0.18) if cuts else 1.0
    values = jax.random.normal(rng, extent, jnp.float32) * deviation * factor_of
    return jnp.minimum(jnp.maximum(values, -reach), reach).astype(dtype)


def setup_inputs(seed: int = 0) -> dict:
    splits = jax.random.split(jax.random.key(seed), 9)
    return {
        "section_inputs": gaussian(splits[0], (N_PIPE * N_DP * TOK_DEV, D), 1.0, 6.0, ((0, 32),)),
        "out_grad": gaussian(splits[1], (N_DP * TOK_DEV, D), 1.0, 6.0, ((0, 8),)),
        "up_weight": gaussian(splits[2], (N_PIPE * FFW, D), D ** -0.5, 0.078125, ((0, 4),)),
        "down_weight": gaussian(splits[3], (N_PIPE * FFW, D), D ** -0.5, 0.078125, ((0, 4),)),
        "momentum": gaussian(splits[4], (N_PIPE * PROWS, D), 0.5, 4.0, ((0, 4),)),
        "worker_error": gaussian(splits[5], (N_PIPE * PROWS, N_DP * D), 0.5, 4.0, ((0, 4), (1, 8))),
        "server_error": gaussian(splits[6], (N_PIPE * PROWS, D), 0.3, 3.0, ((0, 4), (1, 8)), jnp.float32),
        "owner_map": jax.random.permutation(splits[7], N_DP).astype(jnp.int32),
    }


epsilon = 1e-06

def gelu_parts(pre_act):
    activated, pullback = jax.vjp(jax.nn.gelu, pre_act)
    gelu_slope = pullback(jnp.ones_like(pre_act))[0]
    return (activated, gelu_slope)

def reference(section_inputs, out_grad, up_weight, down_weight, momentum, worker_error, server_error, owner_map):
    inputs_all = section_inputs.reshape(N_PIPE, N_DP, TOK_DEV, D)
    up_all = up_weight.reshape(N_PIPE, FFW, D)
    down_all = down_weight.reshape(N_PIPE, FFW, D)
    mom_all = momentum.reshape(N_PIPE, PROWS, D)
    werr_all = worker_error.reshape(N_PIPE, PROWS, N_DP, D)
    serr_all = server_error.reshape(N_PIPE, PROWS, N_DP, CW)
    rank_group = jnp.argsort(owner_map).astype(jnp.int32)
    incoming = out_grad.reshape(N_DP, TOK_DEV, D)
    moms = [None] * N_PIPE
    werrs = [None] * N_PIPE
    serrs = [None] * N_PIPE
    for section in reversed(range(N_PIPE)):
        xin = inputs_all[section].astype(jnp.float32)
        up_f = up_all[section].astype(jnp.float32)
        down_f = down_all[section].astype(jnp.float32)
        pre_act = jnp.einsum('wtd,fd->wtf', xin, up_f)
        activated, gelu_slope = gelu_parts(pre_act)
        act_b = activated.astype(jnp.bfloat16)
        grad_f = incoming.astype(jnp.float32)
        d_act = jnp.einsum('wtd,fd->wtf', grad_f, down_f)
        d_pre = (d_act * gelu_slope).astype(jnp.bfloat16)
        passed = (grad_f + jnp.einsum('wtf,fd->wtd', d_pre.astype(jnp.float32), up_f)).astype(jnp.bfloat16)
        grad_up = jnp.einsum('wtf,wtd->wfd', d_pre.astype(jnp.float32), xin)
        grad_down = jnp.einsum('wtf,wtd->wfd', act_b.astype(jnp.float32), grad_f)
        weight_grads = jnp.concatenate([grad_up, grad_down], axis=1)
        werr = jnp.transpose(werr_all[section], (1, 0, 2)).astype(jnp.float32)
        combined = 0.9 * mom_all[section].astype(jnp.float32)[None] + 0.1 * weight_grads + werr
        blocks = combined.reshape(N_DP, PROWS, N_DP, CW)
        group_scale = lax.optimization_barrier(jnp.mean(jnp.abs(blocks), axis=(1, 3), keepdims=True)) + epsilon
        packed = (group_scale * jnp.tanh(blocks / group_scale)).astype(jnp.bfloat16)
        new_werr = (blocks - packed.astype(jnp.float32)).astype(jnp.bfloat16).reshape(N_DP, PROWS, D)
        werrs[section] = jnp.transpose(new_werr, (1, 0, 2)).reshape(PROWS, N_DP * D)
        average = lax.optimization_barrier(jnp.sum(packed.astype(jnp.float32), axis=0)) / N_DP
        serr_group = jnp.take(serr_all[section], owner_map, axis=1)
        updated = average + serr_group
        server_scale = lax.optimization_barrier(jnp.mean(jnp.abs(updated), axis=(0, 2), keepdims=True)) + epsilon
        server_packed = (server_scale * jnp.tanh(updated / server_scale)).astype(jnp.bfloat16)
        new_serr = updated - server_packed.astype(jnp.float32)
        serrs[section] = jnp.take(new_serr, rank_group, axis=1).reshape(PROWS, D)
        moms[section] = server_packed.reshape(PROWS, D)
        incoming = passed
    return (jnp.concatenate(moms, axis=0), jnp.concatenate(werrs, axis=0), jnp.concatenate(serrs, axis=0))
```

```python
import functools

import jax
import jax.numpy as jnp
from jax import lax
from jax.experimental import pallas as pl
from jax.experimental.pallas import tpu as pltpu
from jax.sharding import PartitionSpec as P

epsilon = 1e-06


def passed_along(block, axis, distance):
    devices = range(lax.axis_size(axis))
    route = [(i - distance, i) for i in devices if i - distance in devices]
    return lax.ppermute(block, axis, route)


def gelu_parts(pre_act):
    activated, pullback = jax.vjp(jax.nn.gelu, pre_act)
    gelu_slope = pullback(jnp.ones_like(pre_act))[0]
    return (activated, gelu_slope)


def backstep(incoming, slope_rows, up_weight, down_weight):
    contract = (((1,), (1,)), ((), ()))
    d_act = lax.dot_general(incoming, down_weight, contract, preferred_element_type=jnp.float32)
    d_pre = (d_act * slope_rows).astype(jnp.bfloat16)
    passed = (
        incoming.astype(jnp.float32) + jnp.dot(d_pre, up_weight, preferred_element_type=jnp.float32)
    ).astype(jnp.bfloat16)
    return (d_pre, passed)


def on_device(
    section_inputs,
    out_grad,
    up_weight,
    down_weight,
    momentum,
    worker_error,
    server_error,
    owner_map,
):
    sections = lax.axis_size("pipe")
    section = lax.axis_index("pipe")
    ranks = lax.axis_size("dp")
    tok_rows = section_inputs.shape[0]
    hidden_units = up_weight.shape[0]
    contract = (((1,), (1,)), ((), ()))
    pre_act = lax.dot_general(
        section_inputs, up_weight, contract, preferred_element_type=jnp.float32
    )
    activated, gelu_slope = gelu_parts(pre_act)
    act_b = activated.astype(jnp.bfloat16)
    kept_grad = jnp.zeros_like(out_grad)
    kept_pre = jnp.zeros((tok_rows, hidden_units), jnp.bfloat16)
    incoming = out_grad
    passed = out_grad
    for turn_number in range(sections):
        if turn_number > 0:
            incoming = passed_along(passed, "pipe", -1)
        d_pre, passed = backstep(incoming, gelu_slope, up_weight, down_weight)
        is_active = section == sections - 1 - turn_number
        kept_grad = jnp.where(is_active, incoming, kept_grad)
        kept_pre = jnp.where(is_active, d_pre, kept_pre)
    token_contract = (((0,), (0,)), ((), ()))
    grad_up = lax.dot_general(
        kept_pre, section_inputs, token_contract, preferred_element_type=jnp.float32
    )
    grad_down = lax.dot_general(
        act_b, kept_grad, token_contract, preferred_element_type=jnp.float32
    )
    weight_grads = jnp.concatenate([grad_up, grad_down], axis=0)
    combined = (
        0.9 * momentum.astype(jnp.float32) + 0.1 * weight_grads + worker_error.astype(jnp.float32)
    )
    param_rows = combined.shape[0]
    group_cols = combined.shape[1] // ranks
    blocks = combined.reshape(param_rows, ranks, group_cols)
    group_scale = jnp.mean(jnp.abs(blocks), axis=(0, 2), keepdims=True) + epsilon
    packed = (group_scale * jnp.tanh(blocks / group_scale)).astype(jnp.bfloat16)
    new_worker = (
        (blocks - packed.astype(jnp.float32))
        .astype(jnp.bfloat16)
        .reshape(param_rows, ranks * group_cols)
    )
    rank_group = jnp.argsort(owner_map)
    outgoing = jnp.take(packed, rank_group, axis=1)
    received = lax.all_to_all(outgoing, "dp", split_axis=1, concat_axis=1, tiled=True)
    average = jnp.sum(received.astype(jnp.float32), axis=1) / ranks
    updated = average + server_error
    server_scale = jnp.mean(jnp.abs(updated)) + epsilon
    server_packed = (server_scale * jnp.tanh(updated / server_scale)).astype(jnp.bfloat16)
    new_server = updated - server_packed.astype(jnp.float32)
    collected = lax.all_gather(server_packed[:, None, :], "dp", axis=1, tiled=True)
    new_momentum = jnp.take(collected, owner_map, axis=1).reshape(param_rows, ranks * group_cols)
    return (new_momentum, new_worker, new_server)


MESH = pl.DeviceIdType.MESH
slope_c = 0.7978845608028654
slope_k = 0.044715
row_step = 32


def fused_kernel(
    group_ref,
    x_hbm,
    g_hbm,
    u_hbm,
    v_hbm,
    m_hbm,
    e_hbm,
    se_hbm,
    mom_out,
    work_out,
    serv_out,
    x_v,
    g_v,
    u_v,
    v_v,
    m_v,
    e_v,
    se_v,
    ups,
    pres,
    act_t,
    slope_v,
    pre_v,
    pre_t,
    dact,
    comb,
    own_pack,
    own_sum,
    work_v,
    sib_out,
    sib_in,
    rs_out,
    rs_in,
    gath,
    in_sem,
    out_sem,
    z_send,
    z_recv,
    up_send,
    up_recv,
    pre_send,
    pre_recv,
    sib_send,
    sib_recv,
    rs_send,
    rs_recv,
    ag_send,
    ag_recv,
):
    sec = lax.axis_index("pipe")
    me = lax.axis_index("dp")
    sections = lax.axis_size("pipe")
    ranks = lax.axis_size("dp")
    toks, width = x_hbm.shape
    units = u_v.shape[0]
    group_cols = width // ranks
    piece = units // ranks
    core = me % 2
    x_bit = (me // 2) % 2
    y_bit = me // 4
    sib = me + 1 - 2 * core
    nbr_x = me + 2 - 4 * x_bit
    nbr_y = me + 4 - 8 * y_bit
    diag = nbr_x + 4 - 8 * y_bit
    flip = 1 - 2 * core
    peers = (nbr_x, nbr_y, diag)

    def remote(src, dst, send, recv, pipe, dp):
        return pltpu.make_async_remote_copy(
            src_ref=src,
            dst_ref=dst,
            send_sem=send,
            recv_sem=recv,
            device_id=(pipe, dp),
            device_id_type=MESH,
        )

    def whole(src, dst, i):
        return [pltpu.make_async_copy(src, dst, in_sem.at[i, 0])]

    def grouped(src, dst, i):
        return [
            pltpu.make_async_copy(
                src.at[:, pl.ds(c * group_cols, group_cols)], dst.at[c], in_sem.at[i, c]
            )
            for c in range(ranks)
        ]

    loads = [
        whole(u_hbm, u_v, 0),
        grouped(x_hbm, x_v, 1),
        whole(v_hbm, v_v, 2),
        grouped(g_hbm, g_v, 3),
        grouped(m_hbm, m_v, 4),
        grouped(e_hbm, e_v, 5),
        whole(se_hbm, se_v, 6),
    ]
    for copies in loads:
        for load in copies:
            load.start()

    def loaded(i):
        for load in loads[i]:
            load.wait()

    barrier = pltpu.get_barrier_semaphore()
    for peer in (sib,) + peers:
        pl.semaphore_signal(barrier, inc=1, device_id=(sec, peer), device_id_type=MESH)
    for hop in range(1, sections):
        pl.semaphore_signal(
            barrier, inc=1, device_id=((sec + hop) % sections, me), device_id_type=MESH
        )
    pl.semaphore_wait(barrier, 3 + sections)

    def up_rows(j, rank):
        return ups.at[j - 1, pl.ds(pl.multiple_of(rank * piece, piece), piece)]

    def own_rows():
        return u_hbm.at[pl.ds(pl.multiple_of(me * piece, piece), piece)]

    def send_up(target):
        dst = ups.at[
            jnp.maximum(sec - 1, 0), pl.ds(pl.multiple_of(me * piece, piece), piece)
        ]
        return remote(own_rows(), dst, z_send.at[target], z_recv.at[jnp.maximum(sec - 1, 0)], target, me)

    for target in range(sections - 1):

        @pl.when(target < sec)
        def _():
            send_up(target).start()

    def spread_copy(place, send, recv, i):
        if i < 3:
            return remote(place(me), place(me), send.at[i], recv.at[i], sec, peers[i])
        source = me if i == 3 else peers[i - 4]
        return remote(place(source), place(source), send.at[i], recv.at[i], sec, sib)

    def arrive(place, send, recv, i):
        source = peers[i] if i < 3 else (me if i == 3 else peers[i - 4]) + flip
        remote(place(source), place(source), send.at[i], recv.at[i], sec, sib).wait_recv()

    def spread_start(place, send, recv):
        for i in (2, 0, 1, 3):
            spread_copy(place, send, recv, i).start()

    def spread_relay(place, send, recv):
        for i in (0, 1, 2):
            arrive(place, send, recv, i)
            spread_copy(place, send, recv, 4 + i).start()

    def spread_finish(place, send, recv):
        for i in (3, 4, 5, 6):
            arrive(place, send, recv, i)

    def spread_drain(place, send, recv):
        for i in range(7):
            spread_copy(place, send, recv, i).wait_send()

    def up_args(j):
        return (lambda rank: up_rows(j, rank), up_send.at[j - 1], up_recv.at[j - 1])

    contract = (((1,), (1,)), ((), ()))
    chunks = ranks

    def cols_of(i):
        return pl.ds(pl.multiple_of(i * group_cols, group_cols), group_cols)

    def contracted(left, right):
        dact[...] = jnp.zeros_like(dact)

        @pl.loop(0, chunks)
        def _(i):
            dact[...] += lax.dot_general(
                left[i],
                right[:, cols_of(i)],
                contract,
                preferred_element_type=jnp.float32,
            )

    loaded(0)
    loaded(1)
    contracted(x_v, u_v)
    pre = dact[...]
    tanh = jnp.tanh(slope_c * (pre + slope_k * (pre * pre * pre)))
    act = 0.5 * pre * (1.0 + tanh)
    act_t[...] = jnp.transpose(act).astype(jnp.bfloat16)
    slope_v[...] = 0.5 * (1.0 + tanh) + (0.5 * slope_c) * pre * (1.0 - tanh * tanh) * (
        1.0 + 3.0 * slope_k * (pre * pre)
    )
    loaded(2)
    loaded(3)

    for j in range(1, sections):

        @pl.when(j > sec)
        def _():
            remote(
                up_rows(j, me), up_rows(j, me), z_send.at[0], z_recv.at[j - 1], sec, sib
            ).wait_recv()
            spread_start(*up_args(j))

    for j in range(1, sections):

        @pl.when(j > sec)
        def _():
            spread_relay(*up_args(j))

    for j in range(sections - 1, 0, -1):

        @pl.when(j > sec)
        def _():
            spread_finish(*up_args(j))
            remote(
                pres.at[j - 1], pres.at[j - 1], pre_send.at[0], pre_recv.at[j - 1], sec, sib
            ).wait_recv()

            @pl.loop(0, chunks)
            def _(i):
                step = jnp.dot(
                    pres[j - 1], ups[j - 1, :, cols_of(i)], preferred_element_type=jnp.float32
                )
                g_v[i] = (g_v[i].astype(jnp.float32) + step).astype(jnp.bfloat16)

    contracted(g_v, v_v)
    d_pre = dact[...] * slope_v[...]
    pre_v[...] = d_pre.astype(jnp.bfloat16)
    pre_t[...] = jnp.transpose(d_pre).astype(jnp.bfloat16)

    def send_pre(target):
        slot = jnp.maximum(sec - 1, 0)
        return remote(pre_v, pres.at[slot], pre_send.at[target], pre_recv.at[slot], target, me)

    for target in range(sections - 2, -1, -1):

        @pl.when(target < sec)
        def _():
            send_pre(target).start()

    for i in (4, 5, 6):
        loaded(i)

    rows = m_hbm.shape[0]
    entries = rows * group_cols
    steps = rows // row_step

    def rows_of(i):
        return pl.ds(pl.multiple_of(i * row_step, row_step), row_step)

    def magnitude(ref):
        def body(i, total):
            return total + jnp.abs(ref[rows_of(i)])

        total = lax.fori_loop(0, steps, body, jnp.zeros((row_step, group_cols), jnp.float32))
        return jnp.sum(total) / entries + epsilon

    def pack(rank, into):
        group = group_ref[rank]
        for half, (weights, values) in enumerate(((pre_t, x_v), (act_t, g_v))):
            part = pl.ds(half * units, units)
            comb[part] = (
                0.9 * m_v[group, part].astype(jnp.float32)
                + 0.1 * jnp.dot(weights[...], values[group], preferred_element_type=jnp.float32)
                + e_v[group, part].astype(jnp.float32)
            )
        scale = magnitude(comb)

        @pl.loop(0, steps)
        def _(i):
            value = comb[rows_of(i)]
            packed = (scale * jnp.tanh(value / scale)).astype(jnp.bfloat16)
            into[rows_of(i)] = packed
            work_v[rank, rows_of(i)] = (value - packed.astype(jnp.float32)).astype(jnp.bfloat16)

        pltpu.make_async_copy(work_v.at[rank], work_out.at[rank], out_sem.at[rank]).start()

    dests = (diag, nbr_x, nbr_y, me)

    def sib_copy(i):
        return remote(sib_out.at[i], sib_in.at[i], sib_send.at[i], sib_recv.at[i], sec, sib)

    def rs_copy(i):
        return remote(rs_out.at[i], rs_in.at[i], rs_send.at[i], rs_recv.at[i], sec, dests[i])

    for i, dest in enumerate(dests):
        pack(dest + flip, sib_out.at[i])
        sib_copy(i).start()
        pack(dest, own_pack)
        sib_copy(i).wait_recv()

        @pl.loop(0, steps)
        def _(k):
            both = own_pack[rows_of(k)].astype(jnp.float32) + sib_in[i, rows_of(k)].astype(
                jnp.float32
            )
            if i < 3:
                rs_out[i, rows_of(k)] = both.astype(jnp.bfloat16)
            else:
                own_sum[rows_of(k)] = both

        if i < 3:
            rs_copy(i).start()

    for i in range(3):
        rs_copy(i).wait_recv()

    @pl.loop(0, steps)
    def _(k):
        total = own_sum[rows_of(k)]
        for i in range(3):
            total = total + rs_in[i, rows_of(k)].astype(jnp.float32)
        comb[rows_of(k)] = total / ranks + se_v[rows_of(k)]

    scale = magnitude(comb)

    @pl.loop(0, steps)
    def _(k):
        value = comb[rows_of(k)]
        packed = (scale * jnp.tanh(value / scale)).astype(jnp.bfloat16)
        gath[me, rows_of(k)] = packed
        own_sum[rows_of(k)] = value - packed.astype(jnp.float32)

    def gath_args():
        return (lambda rank: gath.at[rank], ag_send, ag_recv)

    spread_start(*gath_args())
    serv_copy = pltpu.make_async_copy(own_sum, serv_out, in_sem.at[0, 0])
    serv_copy.start()

    for rank in range(ranks):
        pltpu.make_async_copy(work_v.at[rank], work_out.at[rank], out_sem.at[rank]).wait()
    spread_relay(*gath_args())
    spread_finish(*gath_args())
    serv_copy.wait()
    mom_copy = pltpu.make_async_copy(gath, mom_out, in_sem.at[1, 0])
    mom_copy.start()
    spread_drain(*gath_args())
    for i in range(4):
        sib_copy(i).wait_send()
    for i in range(3):
        rs_copy(i).wait_send()
    for target in range(sections - 1):

        @pl.when(target < sec)
        def _():
            send_up(target).wait_send()
            send_pre(target).wait_send()

    for j in range(1, sections):

        @pl.when(j > sec)
        def _():
            spread_drain(*up_args(j))

    mom_copy.wait()


def place_kernel(owner_ref, mom_ref, work_ref, serv_ref, mom_out, work_out, serv_out):
    mom_out[...] = mom_ref[0]
    work_out[...] = work_ref[0]
    serv_out[...] = serv_ref[...]


def fused_on_device(
    section_inputs,
    out_grad,
    up_weight,
    down_weight,
    momentum,
    worker_error,
    server_error,
    owner_map,
):
    sections = lax.axis_size("pipe")
    ranks = lax.axis_size("dp")
    toks, width = section_inputs.shape
    units = up_weight.shape[0]
    rows = momentum.shape[0]
    group_cols = width // ranks
    bf16, f32 = jnp.bfloat16, jnp.float32
    dma = pltpu.SemaphoreType.DMA
    hbm = pl.BlockSpec(memory_space=pl.ANY)
    block = (rows, group_cols)
    order = jnp.arange(ranks, dtype=jnp.int32)
    rank_group = jnp.sum(jnp.where(owner_map[None, :] == order[:, None], order[None, :], 0), axis=1)
    moms, works, serv = pl.pallas_call(
        fused_kernel,
        out_shape=(
            jax.ShapeDtypeStruct((ranks,) + block, bf16),
            jax.ShapeDtypeStruct((ranks,) + block, bf16),
            jax.ShapeDtypeStruct(block, f32),
        ),
        in_specs=[pl.BlockSpec(memory_space=pltpu.SMEM)] + [hbm] * 7,
        out_specs=(hbm, hbm, hbm),
        scratch_shapes=[
            pltpu.VMEM((ranks, toks, group_cols), bf16),
            pltpu.VMEM((ranks, toks, group_cols), bf16),
            pltpu.VMEM((units, width), bf16),
            pltpu.VMEM((units, width), bf16),
            pltpu.VMEM((ranks,) + block, bf16),
            pltpu.VMEM((ranks,) + block, bf16),
            pltpu.VMEM(block, f32),
            pltpu.VMEM((sections - 1, units, width), bf16),
            pltpu.VMEM((sections - 1, toks, units), bf16),
            pltpu.VMEM((units, toks), bf16),
            pltpu.VMEM((toks, units), f32),
            pltpu.VMEM((toks, units), bf16),
            pltpu.VMEM((units, toks), bf16),
            pltpu.VMEM((toks, units), f32),
            pltpu.VMEM(block, f32),
            pltpu.VMEM(block, bf16),
            pltpu.VMEM(block, f32),
            pltpu.VMEM((ranks,) + block, bf16),
            pltpu.VMEM((4,) + block, bf16),
            pltpu.VMEM((4,) + block, bf16),
            pltpu.VMEM((3,) + block, bf16),
            pltpu.VMEM((3,) + block, bf16),
            pltpu.VMEM((ranks,) + block, bf16),
            dma((7, ranks)),
            dma((ranks,)),
            dma((sections - 1,)),
            dma((sections - 1,)),
            dma((sections - 1, 7)),
            dma((sections - 1, 7)),
            dma((sections - 1,)),
            dma((sections - 1,)),
            dma((4,)),
            dma((4,)),
            dma((3,)),
            dma((3,)),
            dma((7,)),
            dma((7,)),
        ],
        compiler_params=pltpu.CompilerParams(
            collective_id=0, has_side_effects=True, vmem_limit_bytes=56 * 1024 * 1024
        ),
        name="adapter_step",
    )(
        rank_group,
        section_inputs,
        out_grad,
        up_weight,
        down_weight,
        momentum,
        worker_error,
        server_error,
    )
    part = rows // ranks
    return pl.pallas_call(
        place_kernel,
        out_shape=(
            jax.ShapeDtypeStruct((rows, width), bf16),
            jax.ShapeDtypeStruct((rows, width), bf16),
            jax.ShapeDtypeStruct(block, f32),
        ),
        grid_spec=pltpu.PrefetchScalarGridSpec(
            num_scalar_prefetch=1,
            grid=(ranks,),
            in_specs=[
                pl.BlockSpec((1,) + block, lambda c, owner: (owner[c], 0, 0)),
                pl.BlockSpec((1,) + block, lambda c, owner: (owner[c], 0, 0)),
                pl.BlockSpec((part, group_cols), lambda c, owner: (c, 0)),
            ],
            out_specs=[
                pl.BlockSpec(block, lambda c, owner: (0, c)),
                pl.BlockSpec(block, lambda c, owner: (0, c)),
                pl.BlockSpec((part, group_cols), lambda c, owner: (c, 0)),
            ],
        ),
        name="place_groups",
    )(owner_map, moms, works, serv)


def solution(mesh):
    in_specs = (
        P(("pipe", "dp"), None),
        P("dp", None),
        P("pipe", None),
        P("pipe", None),
        P("pipe", None),
        P("pipe", "dp"),
        P("pipe", "dp"),
        P(),
    )
    out_specs = (P("pipe", None), P("pipe", "dp"), P("pipe", "dp"))
    fits = mesh.shape["dp"] == 8 and mesh.shape["pipe"] == 4
    return jax.shard_map(
        fused_on_device if fits else on_device, mesh=mesh, in_specs=in_specs, out_specs=out_specs, check_vma=False
    )
```

```python
import functools

import jax
import jax.numpy as jnp
from jax import lax
from jax.experimental import pallas as pl
from jax.experimental.pallas import tpu as pltpu
from jax.sharding import PartitionSpec as P

epsilon = 1e-06


def passed_along(block, axis, distance):
    devices = range(lax.axis_size(axis))
    route = [(i - distance, i) for i in devices if i - distance in devices]
    return lax.ppermute(block, axis, route)


def gelu_parts(pre_act):
    activated, pullback = jax.vjp(jax.nn.gelu, pre_act)
    gelu_slope = pullback(jnp.ones_like(pre_act))[0]
    return (activated, gelu_slope)


def backstep(incoming, slope_rows, up_weight, down_weight):
    contract = (((1,), (1,)), ((), ()))
    d_act = lax.dot_general(incoming, down_weight, contract, preferred_element_type=jnp.float32)
    d_pre = (d_act * slope_rows).astype(jnp.bfloat16)
    passed = (
        incoming.astype(jnp.float32) + jnp.dot(d_pre, up_weight, preferred_element_type=jnp.float32)
    ).astype(jnp.bfloat16)
    return (d_pre, passed)


def on_device(
    section_inputs,
    out_grad,
    up_weight,
    down_weight,
    momentum,
    worker_error,
    server_error,
    owner_map,
):
    sections = lax.axis_size("pipe")
    section = lax.axis_index("pipe")
    ranks = lax.axis_size("dp")
    tok_rows = section_inputs.shape[0]
    hidden_units = up_weight.shape[0]
    contract = (((1,), (1,)), ((), ()))
    pre_act = lax.dot_general(
        section_inputs, up_weight, contract, preferred_element_type=jnp.float32
    )
    activated, gelu_slope = gelu_parts(pre_act)
    act_b = activated.astype(jnp.bfloat16)
    kept_grad = jnp.zeros_like(out_grad)
    kept_pre = jnp.zeros((tok_rows, hidden_units), jnp.bfloat16)
    incoming = out_grad
    passed = out_grad
    for turn_number in range(sections):
        if turn_number > 0:
            incoming = passed_along(passed, "pipe", -1)
        d_pre, passed = backstep(incoming, gelu_slope, up_weight, down_weight)
        is_active = section == sections - 1 - turn_number
        kept_grad = jnp.where(is_active, incoming, kept_grad)
        kept_pre = jnp.where(is_active, d_pre, kept_pre)
    token_contract = (((0,), (0,)), ((), ()))
    grad_up = lax.dot_general(
        kept_pre, section_inputs, token_contract, preferred_element_type=jnp.float32
    )
    grad_down = lax.dot_general(
        act_b, kept_grad, token_contract, preferred_element_type=jnp.float32
    )
    weight_grads = jnp.concatenate([grad_up, grad_down], axis=0)
    combined = (
        0.9 * momentum.astype(jnp.float32) + 0.1 * weight_grads + worker_error.astype(jnp.float32)
    )
    param_rows = combined.shape[0]
    group_cols = combined.shape[1] // ranks
    blocks = combined.reshape(param_rows, ranks, group_cols)
    group_scale = jnp.mean(jnp.abs(blocks), axis=(0, 2), keepdims=True) + epsilon
    packed = (group_scale * jnp.tanh(blocks / group_scale)).astype(jnp.bfloat16)
    new_worker = (
        (blocks - packed.astype(jnp.float32))
        .astype(jnp.bfloat16)
        .reshape(param_rows, ranks * group_cols)
    )
    rank_group = jnp.argsort(owner_map)
    outgoing = jnp.take(packed, rank_group, axis=1)
    received = lax.all_to_all(outgoing, "dp", split_axis=1, concat_axis=1, tiled=True)
    average = jnp.sum(received.astype(jnp.float32), axis=1) / ranks
    updated = average + server_error
    server_scale = jnp.mean(jnp.abs(updated)) + epsilon
    server_packed = (server_scale * jnp.tanh(updated / server_scale)).astype(jnp.bfloat16)
    new_server = updated - server_packed.astype(jnp.float32)
    collected = lax.all_gather(server_packed[:, None, :], "dp", axis=1, tiled=True)
    new_momentum = jnp.take(collected, owner_map, axis=1).reshape(param_rows, ranks * group_cols)
    return (new_momentum, new_worker, new_server)


MESH = pl.DeviceIdType.MESH
slope_c = 0.7978845608028654
slope_k = 0.044715
row_step = 32
col_step = 256


def fused_kernel(
    group_ref,
    x_hbm,
    g_hbm,
    u_hbm,
    v_hbm,
    m_hbm,
    e_hbm,
    se_hbm,
    mom_out,
    work_out,
    serv_out,
    x_v,
    g_v,
    u_v,
    v_v,
    m_v,
    e_v,
    se_v,
    ups,
    pres,
    act_t,
    slope_v,
    pre_v,
    pre_t,
    dact,
    comb,
    own_pack,
    own_sum,
    work_v,
    sib_out,
    sib_in,
    rs_out,
    rs_in,
    gath,
    in_sem,
    out_sem,
    z_send,
    z_recv,
    up_send,
    up_recv,
    pre_send,
    pre_recv,
    sib_send,
    sib_recv,
    rs_send,
    rs_recv,
    ag_send,
    ag_recv,
):
    sec = lax.axis_index("pipe")
    me = lax.axis_index("dp")
    sections = lax.axis_size("pipe")
    ranks = lax.axis_size("dp")
    toks, width = x_hbm.shape
    units = u_v.shape[0]
    group_cols = width // ranks
    piece = units // ranks
    core = me % 2
    x_bit = (me // 2) % 2
    y_bit = me // 4
    sib = me + 1 - 2 * core
    nbr_x = me + 2 - 4 * x_bit
    nbr_y = me + 4 - 8 * y_bit
    diag = nbr_x + 4 - 8 * y_bit
    flip = 1 - 2 * core
    peers = (nbr_x, nbr_y, diag)

    def remote(src, dst, send, recv, pipe, dp):
        return pltpu.make_async_remote_copy(
            src_ref=src,
            dst_ref=dst,
            send_sem=send,
            recv_sem=recv,
            device_id=(pipe, dp),
            device_id_type=MESH,
        )

    def whole(src, dst, i):
        return [pltpu.make_async_copy(src, dst, in_sem.at[i, 0])]

    def grouped(src, dst, i):
        return [
            pltpu.make_async_copy(
                src.at[:, pl.ds(c * group_cols, group_cols)], dst.at[c], in_sem.at[i, c]
            )
            for c in range(ranks)
        ]

    loads = [
        whole(u_hbm, u_v, 0),
        grouped(x_hbm, x_v, 1),
        whole(v_hbm, v_v, 2),
        grouped(g_hbm, g_v, 3),
        grouped(m_hbm, m_v, 4),
        grouped(e_hbm, e_v, 5),
        whole(se_hbm, se_v, 6),
    ]
    for copies in loads:
        for load in copies:
            load.start()

    def loaded(i):
        for load in loads[i]:
            load.wait()

    barrier = pltpu.get_barrier_semaphore()
    for peer in (sib,) + peers:
        pl.semaphore_signal(barrier, inc=1, device_id=(sec, peer), device_id_type=MESH)
    for hop in range(1, sections):
        pl.semaphore_signal(
            barrier, inc=1, device_id=((sec + hop) % sections, me), device_id_type=MESH
        )
    pl.semaphore_wait(barrier, 3 + sections)

    def up_rows(j, rank, part=None):
        rows = pl.ds(pl.multiple_of(rank * piece, piece), piece)
        if part is None:
            return ups.at[j - 1, rows]
        return ups.at[j - 1, rows, pl.ds(part * (width // 2), width // 2)]

    def z_own(j):
        rows = pl.ds(pl.multiple_of(me * piece, piece), piece)
        return remote(u_hbm.at[rows], up_rows(j, me), z_send.at[j - 1], z_recv.at[j - 1], j - 1, me)

    def z_pass(j):
        return remote(
            up_rows(j, me),
            up_rows(j, me),
            z_send.at[j - 1],
            z_recv.at[j - 1],
            jnp.maximum(sec - 1, 0),
            me,
        )

    for j in range(1, sections):

        @pl.when(sec == j)
        def _():
            z_own(j).start()

    def spread_copy(place, send, recv, i):
        ref, peer = (
            (place(me), nbr_x),
            (place(me), nbr_y),
            (place(nbr_x, 0), nbr_y),
            (place(nbr_y, 1), nbr_x),
            (place(me), sib),
            (place(nbr_x), sib),
            (place(nbr_y), sib),
            (place(diag), sib),
        )[i]
        return remote(ref, ref, send.at[i], recv.at[i], sec, peer)

    def arrive(place, send, recv, i):
        ref = (
            place(nbr_x),
            place(nbr_y),
            place(diag, 0),
            place(diag, 1),
            place(sib),
            place(nbr_x + flip),
            place(nbr_y + flip),
            place(diag + flip),
        )[i]
        remote(ref, ref, send.at[i], recv.at[i], sec, sib).wait_recv()

    def spread_start(*where):
        for i in (0, 1, 4):
            spread_copy(*where, i).start()

    def spread_pass(*where):
        for i in (0, 1):
            arrive(*where, i)
            spread_copy(*where, 2 + i).start()
            spread_copy(*where, 5 + i).start()

    def spread_diag(*where):
        arrive(*where, 2)
        arrive(*where, 3)
        spread_copy(*where, 7).start()

    def spread_finish(*where):
        for i in (4, 5, 6, 7):
            arrive(*where, i)

    def spread_drain(*where):
        for i in range(8):
            spread_copy(*where, i).wait_send()

    def up_args(j):
        return (functools.partial(up_rows, j), up_send.at[j - 1], up_recv.at[j - 1])

    contract = (((1,), (1,)), ((), ()))
    chunks = ranks

    def cols_of(i):
        return pl.ds(pl.multiple_of(i * group_cols, group_cols), group_cols)

    def contracted(left, right):
        dact[...] = jnp.zeros_like(dact)

        @pl.loop(0, chunks)
        def _(i):
            dact[...] += lax.dot_general(
                left[i],
                right[:, cols_of(i)],
                contract,
                preferred_element_type=jnp.float32,
            )

    loaded(0)
    loaded(1)
    contracted(x_v, u_v)
    pre = dact[...]
    tanh = jnp.tanh(slope_c * (pre + slope_k * (pre * pre * pre)))
    act = 0.5 * pre * (1.0 + tanh)
    act_t[...] = jnp.transpose(act).astype(jnp.bfloat16)
    slope_v[...] = 0.5 * (1.0 + tanh) + (0.5 * slope_c) * pre * (1.0 - tanh * tanh) * (
        1.0 + 3.0 * slope_k * (pre * pre)
    )
    loaded(2)
    loaded(3)

    def z_step(j):
        z_pass(j).wait_recv()

        @pl.when(sec > 0)
        def _():
            z_pass(j).start()

        spread_start(*up_args(j))

    turns = []
    for turn in range(1, sections + 3):
        for lag, step in ((3, spread_diag), (2, spread_pass), (0, z_step)):
            turns.append((step, turn - lag))
    for step, j in turns:
        if 1 <= j < sections:

            @pl.when(j > sec)
            def _():
                if step is z_step:
                    z_step(j)
                else:
                    step(*up_args(j))

    for j in range(sections - 1, 0, -1):

        @pl.when(j > sec)
        def _():
            spread_finish(*up_args(j))
            remote(
                pres.at[j - 1], pres.at[j - 1], pre_send.at[0], pre_recv.at[j - 1], sec, sib
            ).wait_recv()

            @pl.loop(0, chunks)
            def _(i):
                step = jnp.dot(
                    pres[j - 1], ups[j - 1, :, cols_of(i)], preferred_element_type=jnp.float32
                )
                g_v[i] = (g_v[i].astype(jnp.float32) + step).astype(jnp.bfloat16)

    contracted(g_v, v_v)
    d_pre = dact[...] * slope_v[...]
    pre_v[...] = d_pre.astype(jnp.bfloat16)
    pre_t[...] = jnp.transpose(d_pre).astype(jnp.bfloat16)

    def send_pre(target):
        slot = jnp.maximum(sec - 1, 0)
        return remote(pre_v, pres.at[slot], pre_send.at[target], pre_recv.at[slot], target, me)

    for target in range(sections - 2, -1, -1):

        @pl.when(target < sec)
        def _():
            send_pre(target).start()

    for i in (4, 5, 6):
        loaded(i)

    rows = m_hbm.shape[0]
    entries = rows * group_cols
    steps = rows // row_step

    def rows_of(i):
        return pl.ds(pl.multiple_of(i * row_step, row_step), row_step)

    def magnitude(ref):
        def body(i, total):
            return total + jnp.abs(ref[rows_of(i)])

        total = lax.fori_loop(0, steps, body, jnp.zeros((row_step, group_cols), jnp.float32))
        return jnp.sum(total) / entries + epsilon

    def pack(rank, into):
        group = group_ref[rank]
        total = jnp.zeros((8, col_step), jnp.float32)
        for half, (weights, values) in enumerate(((pre_t, x_v), (act_t, g_v))):
            part = pl.ds(half * units, units)
            for k in range(group_cols // col_step):
                cols = pl.ds(k * col_step, col_step)
                value = (
                    0.9 * m_v[group, part, cols].astype(jnp.float32)
                    + 0.1
                    * jnp.dot(
                        weights[...], values[group, :, cols], preferred_element_type=jnp.float32
                    )
                    + e_v[group, part, cols].astype(jnp.float32)
                )
                comb[part, cols] = value
                total = total + jnp.sum(
                    jnp.abs(value).reshape(units // 8, 8, col_step), axis=0
                )
        scale = jnp.sum(total) / entries + epsilon
        inverse = 1.0 / scale

        @pl.loop(0, steps)
        def _(i):
            value = comb[rows_of(i)]
            packed = (scale * jnp.tanh(value * inverse)).astype(jnp.bfloat16)
            into[rows_of(i)] = packed
            work_v[rank, rows_of(i)] = (value - packed.astype(jnp.float32)).astype(jnp.bfloat16)

        pltpu.make_async_copy(work_v.at[rank], work_out.at[rank], out_sem.at[rank]).start()

    dests = (diag, nbr_x, nbr_y, me)

    def sib_copy(i):
        return remote(sib_out.at[i], sib_in.at[i], sib_send.at[i], sib_recv.at[i], sec, sib)

    def rs_copy(i):
        return remote(rs_out.at[i], rs_in.at[i], rs_send.at[i], rs_recv.at[i], sec, dests[i])

    for i, dest in enumerate(dests):
        pack(dest + flip, sib_out.at[i])
        sib_copy(i).start()
        pack(dest, own_pack)
        sib_copy(i).wait_recv()

        @pl.loop(0, steps)
        def _(k):
            both = own_pack[rows_of(k)].astype(jnp.float32) + sib_in[i, rows_of(k)].astype(
                jnp.float32
            )
            if i < 3:
                rs_out[i, rows_of(k)] = both.astype(jnp.bfloat16)
            else:
                own_sum[rows_of(k)] = both

        if i < 3:
            rs_copy(i).start()

    for i in range(3):
        rs_copy(i).wait_recv()

    @pl.loop(0, steps)
    def _(k):
        total = own_sum[rows_of(k)]
        for i in range(3):
            total = total + rs_in[i, rows_of(k)].astype(jnp.float32)
        comb[rows_of(k)] = total / ranks + se_v[rows_of(k)]

    scale = magnitude(comb)
    inverse = 1.0 / scale

    @pl.loop(0, steps)
    def _(k):
        value = comb[rows_of(k)]
        packed = (scale * jnp.tanh(value * inverse)).astype(jnp.bfloat16)
        gath[me, rows_of(k)] = packed
        own_sum[rows_of(k)] = value - packed.astype(jnp.float32)

    def gath_place(rank, part=None):
        if part is None:
            return gath.at[rank]
        return gath.at[rank, pl.ds(part * (rows // 2), rows // 2)]

    gath_args = (gath_place, ag_send, ag_recv)
    spread_start(*gath_args)
    serv_copy = pltpu.make_async_copy(own_sum, serv_out, in_sem.at[0, 0])
    serv_copy.start()

    for rank in range(ranks):
        pltpu.make_async_copy(work_v.at[rank], work_out.at[rank], out_sem.at[rank]).wait()
    spread_pass(*gath_args)
    spread_diag(*gath_args)
    spread_finish(*gath_args)
    serv_copy.wait()
    mom_copy = pltpu.make_async_copy(gath, mom_out, in_sem.at[1, 0])
    mom_copy.start()
    spread_drain(*gath_args)
    for i in range(4):
        sib_copy(i).wait_send()
    for i in range(3):
        rs_copy(i).wait_send()
    for target in range(sections - 1):

        @pl.when(target < sec)
        def _():
            send_pre(target).wait_send()

    for j in range(1, sections):

        @pl.when(sec == j)
        def _():
            z_own(j).wait_send()

        @pl.when(j > sec)
        def _():
            spread_drain(*up_args(j))

            @pl.when(sec > 0)
            def _():
                z_pass(j).wait_send()

    mom_copy.wait()


def place_kernel(owner_ref, mom_ref, work_ref, serv_ref, mom_out, work_out, serv_out, sem):
    ranks, rows, cols = mom_ref.shape
    copies = [pltpu.make_async_copy(serv_ref, serv_out, sem.at[2, 0])]
    for c in range(ranks):
        place = pl.ds(c * cols, cols)
        for i, (src, dst) in enumerate(((mom_ref, mom_out), (work_ref, work_out))):
            copies.append(
                pltpu.make_async_copy(src.at[owner_ref[c]], dst.at[:, place], sem.at[i, c])
            )
    for copy in copies:
        copy.start()
    for copy in copies:
        copy.wait()


def fused_on_device(
    section_inputs,
    out_grad,
    up_weight,
    down_weight,
    momentum,
    worker_error,
    server_error,
    owner_map,
):
    sections = lax.axis_size("pipe")
    ranks = lax.axis_size("dp")
    toks, width = section_inputs.shape
    units = up_weight.shape[0]
    rows = momentum.shape[0]
    group_cols = width // ranks
    bf16, f32 = jnp.bfloat16, jnp.float32
    dma = pltpu.SemaphoreType.DMA
    hbm = pl.BlockSpec(memory_space=pl.ANY)
    block = (rows, group_cols)
    order = jnp.arange(ranks, dtype=jnp.int32)
    rank_group = jnp.sum(jnp.where(owner_map[None, :] == order[:, None], order[None, :], 0), axis=1)
    moms, works, serv = pl.pallas_call(
        fused_kernel,
        out_shape=(
            jax.ShapeDtypeStruct((ranks,) + block, bf16),
            jax.ShapeDtypeStruct((ranks,) + block, bf16),
            jax.ShapeDtypeStruct(block, f32),
        ),
        in_specs=[pl.BlockSpec(memory_space=pltpu.SMEM)] + [hbm] * 7,
        out_specs=(hbm, hbm, hbm),
        scratch_shapes=[
            pltpu.VMEM((ranks, toks, group_cols), bf16),
            pltpu.VMEM((ranks, toks, group_cols), bf16),
            pltpu.VMEM((units, width), bf16),
            pltpu.VMEM((units, width), bf16),
            pltpu.VMEM((ranks,) + block, bf16),
            pltpu.VMEM((ranks,) + block, bf16),
            pltpu.VMEM(block, f32),
            pltpu.VMEM((sections - 1, units, width), bf16),
            pltpu.VMEM((sections - 1, toks, units), bf16),
            pltpu.VMEM((units, toks), bf16),
            pltpu.VMEM((toks, units), f32),
            pltpu.VMEM((toks, units), bf16),
            pltpu.VMEM((units, toks), bf16),
            pltpu.VMEM((toks, units), f32),
            pltpu.VMEM(block, f32),
            pltpu.VMEM(block, bf16),
            pltpu.VMEM(block, f32),
            pltpu.VMEM((ranks,) + block, bf16),
            pltpu.VMEM((4,) + block, bf16),
            pltpu.VMEM((4,) + block, bf16),
            pltpu.VMEM((3,) + block, bf16),
            pltpu.VMEM((3,) + block, bf16),
            pltpu.VMEM((ranks,) + block, bf16),
            dma((7, ranks)),
            dma((ranks,)),
            dma((sections - 1,)),
            dma((sections - 1,)),
            dma((sections - 1, 8)),
            dma((sections - 1, 8)),
            dma((sections - 1,)),
            dma((sections - 1,)),
            dma((4,)),
            dma((4,)),
            dma((3,)),
            dma((3,)),
            dma((8,)),
            dma((8,)),
        ],
        compiler_params=pltpu.CompilerParams(
            collective_id=0, has_side_effects=True, vmem_limit_bytes=56 * 1024 * 1024
        ),
        name="adapter_step",
    )(
        rank_group,
        section_inputs,
        out_grad,
        up_weight,
        down_weight,
        momentum,
        worker_error,
        server_error,
    )
    return pl.pallas_call(
        place_kernel,
        out_shape=(
            jax.ShapeDtypeStruct((rows, width), bf16),
            jax.ShapeDtypeStruct((rows, width), bf16),
            jax.ShapeDtypeStruct(block, f32),
        ),
        in_specs=[pl.BlockSpec(memory_space=pltpu.SMEM), hbm, hbm, hbm],
        out_specs=(hbm, hbm, hbm),
        scratch_shapes=[dma((3, ranks))],
        name="place_groups",
    )(owner_map, moms, works, serv)


def solution(mesh):
    in_specs = (
        P(("pipe", "dp"), None),
        P("dp", None),
        P("pipe", None),
        P("pipe", None),
        P("pipe", None),
        P("pipe", "dp"),
        P("pipe", "dp"),
        P(),
    )
    out_specs = (P("pipe", None), P("pipe", "dp"), P("pipe", "dp"))
    fits = mesh.shape["dp"] == 8 and mesh.shape["pipe"] == 4
    return jax.shard_map(
        fused_on_device if fits else on_device, mesh=mesh, in_specs=in_specs, out_specs=out_specs, check_vma=False
    )
```

```python
import functools

import jax
import jax.numpy as jnp
from jax import lax
from jax.experimental import pallas as pl
from jax.experimental.pallas import tpu as pltpu
from jax.sharding import PartitionSpec as P

epsilon = 1e-06


def passed_along(block, axis, distance):
    devices = range(lax.axis_size(axis))
    route = [(i - distance, i) for i in devices if i - distance in devices]
    return lax.ppermute(block, axis, route)


def gelu_parts(pre_act):
    activated, pullback = jax.vjp(jax.nn.gelu, pre_act)
    gelu_slope = pullback(jnp.ones_like(pre_act))[0]
    return (activated, gelu_slope)


def backstep(incoming, slope_rows, up_weight, down_weight):
    contract = (((1,), (1,)), ((), ()))
    d_act = lax.dot_general(incoming, down_weight, contract, preferred_element_type=jnp.float32)
    d_pre = (d_act * slope_rows).astype(jnp.bfloat16)
    passed = (
        incoming.astype(jnp.float32) + jnp.dot(d_pre, up_weight, preferred_element_type=jnp.float32)
    ).astype(jnp.bfloat16)
    return (d_pre, passed)


def on_device(
    section_inputs,
    out_grad,
    up_weight,
    down_weight,
    momentum,
    worker_error,
    server_error,
    owner_map,
):
    sections = lax.axis_size("pipe")
    section = lax.axis_index("pipe")
    ranks = lax.axis_size("dp")
    tok_rows = section_inputs.shape[0]
    hidden_units = up_weight.shape[0]
    contract = (((1,), (1,)), ((), ()))
    pre_act = lax.dot_general(
        section_inputs, up_weight, contract, preferred_element_type=jnp.float32
    )
    activated, gelu_slope = gelu_parts(pre_act)
    act_b = activated.astype(jnp.bfloat16)
    kept_grad = jnp.zeros_like(out_grad)
    kept_pre = jnp.zeros((tok_rows, hidden_units), jnp.bfloat16)
    incoming = out_grad
    passed = out_grad
    for turn_number in range(sections):
        if turn_number > 0:
            incoming = passed_along(passed, "pipe", -1)
        d_pre, passed = backstep(incoming, gelu_slope, up_weight, down_weight)
        is_active = section == sections - 1 - turn_number
        kept_grad = jnp.where(is_active, incoming, kept_grad)
        kept_pre = jnp.where(is_active, d_pre, kept_pre)
    token_contract = (((0,), (0,)), ((), ()))
    grad_up = lax.dot_general(
        kept_pre, section_inputs, token_contract, preferred_element_type=jnp.float32
    )
    grad_down = lax.dot_general(
        act_b, kept_grad, token_contract, preferred_element_type=jnp.float32
    )
    weight_grads = jnp.concatenate([grad_up, grad_down], axis=0)
    combined = (
        0.9 * momentum.astype(jnp.float32) + 0.1 * weight_grads + worker_error.astype(jnp.float32)
    )
    param_rows = combined.shape[0]
    group_cols = combined.shape[1] // ranks
    blocks = combined.reshape(param_rows, ranks, group_cols)
    group_scale = jnp.mean(jnp.abs(blocks), axis=(0, 2), keepdims=True) + epsilon
    packed = (group_scale * jnp.tanh(blocks / group_scale)).astype(jnp.bfloat16)
    new_worker = (
        (blocks - packed.astype(jnp.float32))
        .astype(jnp.bfloat16)
        .reshape(param_rows, ranks * group_cols)
    )
    rank_group = jnp.argsort(owner_map)
    outgoing = jnp.take(packed, rank_group, axis=1)
    received = lax.all_to_all(outgoing, "dp", split_axis=1, concat_axis=1, tiled=True)
    average = jnp.sum(received.astype(jnp.float32), axis=1) / ranks
    updated = average + server_error
    server_scale = jnp.mean(jnp.abs(updated)) + epsilon
    server_packed = (server_scale * jnp.tanh(updated / server_scale)).astype(jnp.bfloat16)
    new_server = updated - server_packed.astype(jnp.float32)
    collected = lax.all_gather(server_packed[:, None, :], "dp", axis=1, tiled=True)
    new_momentum = jnp.take(collected, owner_map, axis=1).reshape(param_rows, ranks * group_cols)
    return (new_momentum, new_worker, new_server)


MESH = pl.DeviceIdType.MESH
slope_c = 0.7978845608028654
slope_k = 0.044715
row_step = 32
col_step = 256
ag_chunks = 4


def fused_kernel(
    group_ref,
    x_hbm,
    g_hbm,
    u_hbm,
    v_hbm,
    m_hbm,
    e_hbm,
    se_hbm,
    mom_out,
    work_out,
    serv_out,
    x_v,
    g_v,
    u_v,
    v_v,
    m_v,
    e_v,
    se_v,
    ups,
    pres,
    act_t,
    slope_v,
    pre_v,
    pre_t,
    dact,
    mixed,
    comb,
    own_pack,
    own_sum,
    work_v,
    sib_out,
    sib_in,
    rs_out,
    rs_in,
    gath,
    in_sem,
    out_sem,
    z_send,
    z_recv,
    up_send,
    up_recv,
    pre_send,
    pre_recv,
    sib_send,
    sib_recv,
    rs_send,
    rs_recv,
    ag_send,
    ag_recv,
):
    sec = lax.axis_index("pipe")
    me = lax.axis_index("dp")
    sections = lax.axis_size("pipe")
    ranks = lax.axis_size("dp")
    toks, width = x_hbm.shape
    units = u_v.shape[0]
    group_cols = width // ranks
    piece = units // ranks
    core = me % 2
    x_bit = (me // 2) % 2
    y_bit = me // 4
    sib = me + 1 - 2 * core
    nbr_x = me + 2 - 4 * x_bit
    nbr_y = me + 4 - 8 * y_bit
    diag = nbr_x + 4 - 8 * y_bit
    flip = 1 - 2 * core
    peers = (nbr_x, nbr_y, diag)

    def remote(src, dst, send, recv, pipe, dp):
        return pltpu.make_async_remote_copy(
            src_ref=src,
            dst_ref=dst,
            send_sem=send,
            recv_sem=recv,
            device_id=(pipe, dp),
            device_id_type=MESH,
        )

    def whole(src, dst, i):
        return [pltpu.make_async_copy(src, dst, in_sem.at[i, 0])]

    def grouped(src, dst, i):
        return [
            pltpu.make_async_copy(
                src.at[:, pl.ds(c * group_cols, group_cols)], dst.at[c], in_sem.at[i, c]
            )
            for c in range(ranks)
        ]

    loads = [
        whole(u_hbm, u_v, 0),
        grouped(x_hbm, x_v, 1),
        whole(v_hbm, v_v, 2),
        grouped(g_hbm, g_v, 3),
        grouped(m_hbm, m_v, 4),
        grouped(e_hbm, e_v, 5),
        whole(se_hbm, se_v, 6),
    ]
    for copies in loads:
        for load in copies:
            load.start()

    def loaded(i):
        for load in loads[i]:
            load.wait()

    barrier = pltpu.get_barrier_semaphore()
    for peer in (sib,) + peers:
        pl.semaphore_signal(barrier, inc=1, device_id=(sec, peer), device_id_type=MESH)
    for hop in range(1, sections):
        pl.semaphore_signal(
            barrier, inc=1, device_id=((sec + hop) % sections, me), device_id_type=MESH
        )
    pl.semaphore_wait(barrier, 3 + sections)

    def up_rows(j, rank, part=None):
        rows = pl.ds(pl.multiple_of(rank * piece, piece), piece)
        if part is None:
            return ups.at[j - 1, rows]
        return ups.at[j - 1, rows, pl.ds(part * (width // 2), width // 2)]

    def z_own(j):
        rows = pl.ds(pl.multiple_of(me * piece, piece), piece)
        return remote(u_hbm.at[rows], up_rows(j, me), z_send.at[j - 1], z_recv.at[j - 1], j - 1, me)

    def z_pass(j):
        return remote(
            up_rows(j, me),
            up_rows(j, me),
            z_send.at[j - 1],
            z_recv.at[j - 1],
            jnp.maximum(sec - 1, 0),
            me,
        )

    for j in range(1, sections):

        @pl.when(sec == j)
        def _():
            z_own(j).start()

    def spread_copy(place, send, recv, i):
        ref, peer = (
            (place(me), nbr_x),
            (place(me), nbr_y),
            (place(nbr_x, 0), nbr_y),
            (place(nbr_y, 1), nbr_x),
            (place(me), sib),
            (place(nbr_x), sib),
            (place(nbr_y), sib),
            (place(diag), sib),
        )[i]
        return remote(ref, ref, send.at[i], recv.at[i], sec, peer)

    def arrive(place, send, recv, i):
        ref = (
            place(nbr_x),
            place(nbr_y),
            place(diag, 0),
            place(diag, 1),
            place(sib),
            place(nbr_x + flip),
            place(nbr_y + flip),
            place(diag + flip),
        )[i]
        remote(ref, ref, send.at[i], recv.at[i], sec, sib).wait_recv()

    def spread_start(*where):
        for i in (0, 1, 4):
            spread_copy(*where, i).start()

    def spread_pass(*where):
        for i in (0, 1):
            arrive(*where, i)
            spread_copy(*where, 2 + i).start()
            spread_copy(*where, 5 + i).start()

    def spread_diag(*where):
        arrive(*where, 2)
        arrive(*where, 3)
        spread_copy(*where, 7).start()

    def spread_finish(*where):
        for i in (4, 5, 6, 7):
            arrive(*where, i)

    def spread_drain(*where):
        for i in range(8):
            spread_copy(*where, i).wait_send()

    def up_args(j):
        return (functools.partial(up_rows, j), up_send.at[j - 1], up_recv.at[j - 1])

    contract = (((1,), (1,)), ((), ()))
    chunks = ranks

    def cols_of(i):
        return pl.ds(pl.multiple_of(i * group_cols, group_cols), group_cols)

    def contracted(left, right):
        total = jnp.zeros((toks, units), jnp.float32)
        for i in range(chunks):
            total = total + lax.dot_general(
                left(i),
                right[:, cols_of(i)],
                contract,
                preferred_element_type=jnp.float32,
            )
        return total

    def z_step(j):
        z_pass(j).wait_recv()

        @pl.when(sec > 0)
        def _():
            z_pass(j).start()

        spread_start(*up_args(j))

    above = sections - 1 - sec

    def turn(step, k):
        @pl.when(k <= above)
        def _():
            if step is z_step:
                z_step(sec + k)
            else:
                step(*up_args(sec + k))

    turn(z_step, 1)
    loaded(0)
    loaded(1)
    pre = contracted(lambda i: x_v[i], u_v)
    tanh = jnp.tanh(slope_c * (pre + slope_k * (pre * pre * pre)))
    act = 0.5 * pre * (1.0 + tanh)
    act_t[...] = jnp.transpose(act).astype(jnp.bfloat16)
    slope_v[...] = 0.5 * (1.0 + tanh) + (0.5 * slope_c) * pre * (1.0 - tanh * tanh) * (
        1.0 + 3.0 * slope_k * (pre * pre)
    )
    turn(z_step, 2)
    loaded(2)
    loaded(3)
    dact[...] = contracted(lambda i: g_v[i], v_v)
    turn(spread_pass, 1)
    turn(z_step, 3)
    turn(spread_diag, 1)
    turn(spread_pass, 2)

    def cross(k):
        @pl.when(k <= above)
        def _():
            spread_finish(*up_args(sec + k))
            slot = sec + k - 1
            mixed[slot] = contracted(lambda i: ups[slot, :, cols_of(i)], v_v)

    cross(1)
    turn(spread_diag, 2)
    turn(spread_pass, 3)
    cross(2)
    turn(spread_diag, 3)
    cross(3)

    for k in range(sections - 1, 0, -1):

        @pl.when(k <= above)
        def _():
            slot = sec + k - 1
            remote(
                pres.at[slot], pres.at[slot], pre_send.at[0], pre_recv.at[slot], sec, sib
            ).wait_recv()
            dact[...] += jnp.dot(
                pres[slot].astype(jnp.float32), mixed[slot], precision=lax.Precision.HIGHEST
            )

    d_pre = dact[...] * slope_v[...]
    pre_v[...] = d_pre.astype(jnp.bfloat16)
    pre_t[...] = jnp.transpose(d_pre).astype(jnp.bfloat16)

    def send_pre(target):
        slot = jnp.maximum(sec - 1, 0)
        return remote(pre_v, pres.at[slot], pre_send.at[target], pre_recv.at[slot], target, me)

    for target in range(sections - 2, -1, -1):

        @pl.when(target < sec)
        def _():
            send_pre(target).start()

    for low in range(sections - 1):

        @pl.when(sec == low)
        def _():
            @pl.loop(0, chunks)
            def _(i):
                wide = jnp.concatenate([pres[k] for k in range(low, sections - 1)], axis=1)
                tall = ups[low:, :, cols_of(i)].reshape((sections - 1 - low) * units, group_cols)
                step = jnp.dot(wide, tall, preferred_element_type=jnp.float32)
                g_v[i] = (g_v[i].astype(jnp.float32) + step).astype(jnp.bfloat16)

    for i in (4, 5, 6):
        loaded(i)

    rows = m_hbm.shape[0]
    entries = rows * group_cols
    steps = rows // row_step

    def rows_of(i):
        return pl.ds(pl.multiple_of(i * row_step, row_step), row_step)

    def magnitude(ref):
        def body(i, total):
            return total + jnp.abs(ref[rows_of(i)])

        total = lax.fori_loop(0, steps, body, jnp.zeros((row_step, group_cols), jnp.float32))
        return jnp.sum(total) / entries + epsilon

    def pack(rank, into):
        group = group_ref[rank]
        total = jnp.zeros((8, col_step), jnp.float32)
        for half, (weights, values) in enumerate(((pre_t, x_v), (act_t, g_v))):
            part = pl.ds(half * units, units)
            for k in range(group_cols // col_step):
                cols = pl.ds(k * col_step, col_step)
                value = (
                    0.9 * m_v[group, part, cols].astype(jnp.float32)
                    + 0.1
                    * jnp.dot(
                        weights[...], values[group, :, cols], preferred_element_type=jnp.float32
                    )
                    + e_v[group, part, cols].astype(jnp.float32)
                )
                comb[part, cols] = value
                total = total + jnp.sum(
                    jnp.abs(value).reshape(units // 8, 8, col_step), axis=0
                )
        scale = jnp.sum(total) / entries + epsilon
        inverse = 1.0 / scale

        @pl.loop(0, steps)
        def _(i):
            value = comb[rows_of(i)]
            packed = (scale * jnp.tanh(value * inverse)).astype(jnp.bfloat16)
            into[rows_of(i)] = packed
            work_v[rank, rows_of(i)] = (value - packed.astype(jnp.float32)).astype(jnp.bfloat16)

        pltpu.make_async_copy(work_v.at[rank], work_out.at[rank], out_sem.at[rank]).start()

    dests = (diag, nbr_x, nbr_y, me)

    def sib_copy(i):
        return remote(sib_out.at[i], sib_in.at[i], sib_send.at[i], sib_recv.at[i], sec, sib)

    def rs_copy(i):
        return remote(rs_out.at[i], rs_in.at[i], rs_send.at[i], rs_recv.at[i], sec, dests[i])

    for i, dest in enumerate(dests):
        pack(dest + flip, sib_out.at[i])
        sib_copy(i).start()
        pack(dest, own_pack)
        sib_copy(i).wait_recv()

        @pl.loop(0, steps)
        def _(k):
            both = own_pack[rows_of(k)].astype(jnp.float32) + sib_in[i, rows_of(k)].astype(
                jnp.float32
            )
            if i < 3:
                rs_out[i, rows_of(k)] = both.astype(jnp.bfloat16)
            else:
                own_sum[rows_of(k)] = both

        if i < 3:
            rs_copy(i).start()

    for i in range(3):
        rs_copy(i).wait_recv()

    @pl.loop(0, steps)
    def _(k):
        total = own_sum[rows_of(k)]
        for i in range(3):
            total = total + rs_in[i, rows_of(k)].astype(jnp.float32)
        comb[rows_of(k)] = total / ranks + se_v[rows_of(k)]

    scale = magnitude(comb)
    inverse = 1.0 / scale

    @pl.loop(0, steps)
    def _(k):
        value = comb[rows_of(k)]
        packed = (scale * jnp.tanh(value * inverse)).astype(jnp.bfloat16)
        gath[me, rows_of(k)] = packed
        own_sum[rows_of(k)] = value - packed.astype(jnp.float32)

    def gath_place(t, rank, part=None):
        size = rows // ag_chunks
        if part is None:
            return gath.at[rank, pl.ds(t * size, size)]
        return gath.at[rank, pl.ds(t * size + part * (size // 2), size // 2)]

    def ag_args(t):
        return (functools.partial(gath_place, t), ag_send.at[t], ag_recv.at[t])

    for t in range(ag_chunks):
        spread_start(*ag_args(t))

    def keep(i, rank):
        return pltpu.make_async_copy(gath.at[rank], mom_out.at[rank], in_sem.at[1, i])

    kept = (me, nbr_x, nbr_y, diag, sib, nbr_x + flip, nbr_y + flip, diag + flip)
    keep(0, me).start()
    serv_copy = pltpu.make_async_copy(own_sum, serv_out, in_sem.at[0, 0])
    serv_copy.start()

    for rank in range(ranks):
        pltpu.make_async_copy(work_v.at[rank], work_out.at[rank], out_sem.at[rank]).wait()
    for t in range(ag_chunks + 1):
        if t < ag_chunks:
            spread_pass(*ag_args(t))
        if t > 0:
            spread_diag(*ag_args(t - 1))
    for i in (1, 2, 3):
        keep(i, kept[i]).start()
    serv_copy.wait()
    for i in (4, 5, 6, 7):
        for t in range(ag_chunks):
            arrive(*ag_args(t), i)
        keep(i, kept[i]).start()
    for t in range(ag_chunks):
        spread_drain(*ag_args(t))
    for i in range(4):
        sib_copy(i).wait_send()
    for i in range(3):
        rs_copy(i).wait_send()
    for target in range(sections - 1):

        @pl.when(target < sec)
        def _():
            send_pre(target).wait_send()

    for j in range(1, sections):

        @pl.when(sec == j)
        def _():
            z_own(j).wait_send()

        @pl.when(j > sec)
        def _():
            spread_drain(*up_args(j))

            @pl.when(sec > 0)
            def _():
                z_pass(j).wait_send()

    for i in range(8):
        keep(i, kept[i]).wait()


def place_kernel(
    owner_ref, mom_ref, work_ref, serv_ref, mom_out, work_out, serv_out, held, kept, load_sem, store_sem
):
    ranks, rows, cols = mom_ref.shape
    loads = [pltpu.make_async_copy(serv_ref, kept, load_sem.at[2, 0])]
    stores = [pltpu.make_async_copy(kept, serv_out, store_sem.at[2, 0])]
    for i, (src, dst) in enumerate(((work_ref, work_out), (mom_ref, mom_out))):
        for c in range(ranks):
            loads.append(
                pltpu.make_async_copy(src.at[owner_ref[c]], held.at[i, c], load_sem.at[i, c])
            )
            stores.append(
                pltpu.make_async_copy(
                    held.at[i, c], dst.at[:, pl.ds(c * cols, cols)], store_sem.at[i, c]
                )
            )
    for load in loads:
        load.start()
    for load, store in zip(loads, stores):
        load.wait()
        store.start()
    for store in stores:
        store.wait()


def fused_on_device(
    section_inputs,
    out_grad,
    up_weight,
    down_weight,
    momentum,
    worker_error,
    server_error,
    owner_map,
):
    sections = lax.axis_size("pipe")
    ranks = lax.axis_size("dp")
    toks, width = section_inputs.shape
    units = up_weight.shape[0]
    rows = momentum.shape[0]
    group_cols = width // ranks
    bf16, f32 = jnp.bfloat16, jnp.float32
    dma = pltpu.SemaphoreType.DMA
    hbm = pl.BlockSpec(memory_space=pl.ANY)
    block = (rows, group_cols)
    order = jnp.arange(ranks, dtype=jnp.int32)
    rank_group = jnp.sum(jnp.where(owner_map[None, :] == order[:, None], order[None, :], 0), axis=1)
    moms, works, serv = pl.pallas_call(
        fused_kernel,
        out_shape=(
            jax.ShapeDtypeStruct((ranks,) + block, bf16),
            jax.ShapeDtypeStruct((ranks,) + block, bf16),
            jax.ShapeDtypeStruct(block, f32),
        ),
        in_specs=[pl.BlockSpec(memory_space=pltpu.SMEM)] + [hbm] * 7,
        out_specs=(hbm, hbm, hbm),
        scratch_shapes=[
            pltpu.VMEM((ranks, toks, group_cols), bf16),
            pltpu.VMEM((ranks, toks, group_cols), bf16),
            pltpu.VMEM((units, width), bf16),
            pltpu.VMEM((units, width), bf16),
            pltpu.VMEM((ranks,) + block, bf16),
            pltpu.VMEM((ranks,) + block, bf16),
            pltpu.VMEM(block, f32),
            pltpu.VMEM((sections - 1, units, width), bf16),
            pltpu.VMEM((sections - 1, toks, units), bf16),
            pltpu.VMEM((units, toks), bf16),
            pltpu.VMEM((toks, units), f32),
            pltpu.VMEM((toks, units), bf16),
            pltpu.VMEM((units, toks), bf16),
            pltpu.VMEM((toks, units), f32),
            pltpu.VMEM((sections - 1, units, units), f32),
            pltpu.VMEM(block, f32),
            pltpu.VMEM(block, bf16),
            pltpu.VMEM(block, f32),
            pltpu.VMEM((ranks,) + block, bf16),
            pltpu.VMEM((4,) + block, bf16),
            pltpu.VMEM((4,) + block, bf16),
            pltpu.VMEM((3,) + block, bf16),
            pltpu.VMEM((3,) + block, bf16),
            pltpu.VMEM((ranks,) + block, bf16),
            dma((7, ranks)),
            dma((ranks,)),
            dma((sections - 1,)),
            dma((sections - 1,)),
            dma((sections - 1, 8)),
            dma((sections - 1, 8)),
            dma((sections - 1,)),
            dma((sections - 1,)),
            dma((4,)),
            dma((4,)),
            dma((3,)),
            dma((3,)),
            dma((ag_chunks, 8)),
            dma((ag_chunks, 8)),
        ],
        compiler_params=pltpu.CompilerParams(
            collective_id=0, has_side_effects=True, vmem_limit_bytes=56 * 1024 * 1024
        ),
        name="adapter_step",
    )(
        rank_group,
        section_inputs,
        out_grad,
        up_weight,
        down_weight,
        momentum,
        worker_error,
        server_error,
    )
    return pl.pallas_call(
        place_kernel,
        out_shape=(
            jax.ShapeDtypeStruct((rows, width), bf16),
            jax.ShapeDtypeStruct((rows, width), bf16),
            jax.ShapeDtypeStruct(block, f32),
        ),
        in_specs=[pl.BlockSpec(memory_space=pltpu.SMEM), hbm, hbm, hbm],
        out_specs=(hbm, hbm, hbm),
        scratch_shapes=[
            pltpu.VMEM((2, ranks) + block, bf16),
            pltpu.VMEM(block, f32),
            dma((3, ranks)),
            dma((3, ranks)),
        ],
        compiler_params=pltpu.CompilerParams(vmem_limit_bytes=60 * 1024 * 1024),
        name="place_groups",
    )(owner_map, moms, works, serv)


def solution(mesh):
    in_specs = (
        P(("pipe", "dp"), None),
        P("dp", None),
        P("pipe", None),
        P("pipe", None),
        P("pipe", None),
        P("pipe", "dp"),
        P("pipe", "dp"),
        P(),
    )
    out_specs = (P("pipe", None), P("pipe", "dp"), P("pipe", "dp"))
    fits = mesh.shape["dp"] == 8 and mesh.shape["pipe"] == 4
    return jax.shard_map(
        fused_on_device if fits else on_device, mesh=mesh, in_specs=in_specs, out_specs=out_specs, check_vma=False
    )
```

```python
import functools

import jax
import jax.numpy as jnp
from jax import lax
from jax.experimental import pallas as pl
from jax.experimental.pallas import tpu as pltpu
from jax.sharding import PartitionSpec as P

epsilon = 1e-06


def passed_along(block, axis, distance):
    devices = range(lax.axis_size(axis))
    route = [(i - distance, i) for i in devices if i - distance in devices]
    return lax.ppermute(block, axis, route)


def gelu_parts(pre_act):
    activated, pullback = jax.vjp(jax.nn.gelu, pre_act)
    gelu_slope = pullback(jnp.ones_like(pre_act))[0]
    return (activated, gelu_slope)


def backstep(incoming, slope_rows, up_weight, down_weight):
    contract = (((1,), (1,)), ((), ()))
    d_act = lax.dot_general(incoming, down_weight, contract, preferred_element_type=jnp.float32)
    d_pre = (d_act * slope_rows).astype(jnp.bfloat16)
    passed = (
        incoming.astype(jnp.float32) + jnp.dot(d_pre, up_weight, preferred_element_type=jnp.float32)
    ).astype(jnp.bfloat16)
    return (d_pre, passed)


def on_device(
    section_inputs,
    out_grad,
    up_weight,
    down_weight,
    momentum,
    worker_error,
    server_error,
    owner_map,
):
    sections = lax.axis_size("pipe")
    section = lax.axis_index("pipe")
    ranks = lax.axis_size("dp")
    tok_rows = section_inputs.shape[0]
    hidden_units = up_weight.shape[0]
    contract = (((1,), (1,)), ((), ()))
    pre_act = lax.dot_general(
        section_inputs, up_weight, contract, preferred_element_type=jnp.float32
    )
    activated, gelu_slope = gelu_parts(pre_act)
    act_b = activated.astype(jnp.bfloat16)
    kept_grad = jnp.zeros_like(out_grad)
    kept_pre = jnp.zeros((tok_rows, hidden_units), jnp.bfloat16)
    incoming = out_grad
    passed = out_grad
    for turn_number in range(sections):
        if turn_number > 0:
            incoming = passed_along(passed, "pipe", -1)
        d_pre, passed = backstep(incoming, gelu_slope, up_weight, down_weight)
        is_active = section == sections - 1 - turn_number
        kept_grad = jnp.where(is_active, incoming, kept_grad)
        kept_pre = jnp.where(is_active, d_pre, kept_pre)
    token_contract = (((0,), (0,)), ((), ()))
    grad_up = lax.dot_general(
        kept_pre, section_inputs, token_contract, preferred_element_type=jnp.float32
    )
    grad_down = lax.dot_general(
        act_b, kept_grad, token_contract, preferred_element_type=jnp.float32
    )
    weight_grads = jnp.concatenate([grad_up, grad_down], axis=0)
    combined = (
        0.9 * momentum.astype(jnp.float32) + 0.1 * weight_grads + worker_error.astype(jnp.float32)
    )
    param_rows = combined.shape[0]
    group_cols = combined.shape[1] // ranks
    blocks = combined.reshape(param_rows, ranks, group_cols)
    group_scale = jnp.mean(jnp.abs(blocks), axis=(0, 2), keepdims=True) + epsilon
    packed = (group_scale * jnp.tanh(blocks / group_scale)).astype(jnp.bfloat16)
    new_worker = (
        (blocks - packed.astype(jnp.float32))
        .astype(jnp.bfloat16)
        .reshape(param_rows, ranks * group_cols)
    )
    rank_group = jnp.argsort(owner_map)
    outgoing = jnp.take(packed, rank_group, axis=1)
    received = lax.all_to_all(outgoing, "dp", split_axis=1, concat_axis=1, tiled=True)
    average = jnp.sum(received.astype(jnp.float32), axis=1) / ranks
    updated = average + server_error
    server_scale = jnp.mean(jnp.abs(updated)) + epsilon
    server_packed = (server_scale * jnp.tanh(updated / server_scale)).astype(jnp.bfloat16)
    new_server = updated - server_packed.astype(jnp.float32)
    collected = lax.all_gather(server_packed[:, None, :], "dp", axis=1, tiled=True)
    new_momentum = jnp.take(collected, owner_map, axis=1).reshape(param_rows, ranks * group_cols)
    return (new_momentum, new_worker, new_server)


MESH = pl.DeviceIdType.MESH
slope_c = 0.7978845608028654
slope_k = 0.044715
row_step = 32
col_step = 256
ag_chunks = 4


def fused_kernel(
    group_ref,
    x_hbm,
    g_hbm,
    u_hbm,
    v_hbm,
    m_hbm,
    e_hbm,
    se_hbm,
    mom_out,
    work_out,
    serv_out,
    x_v,
    g_v,
    u_v,
    v_v,
    m_v,
    e_v,
    se_v,
    ups,
    pres,
    act_t,
    slope_v,
    pre_v,
    pre_t,
    dact,
    mixed,
    comb,
    own_pack,
    own_sum,
    work_v,
    sib_out,
    sib_in,
    rs_out,
    rs_in,
    gath,
    in_sem,
    out_sem,
    z_send,
    z_recv,
    zd_send,
    zd_recv,
    up_send,
    up_recv,
    pre_send,
    pre_recv,
    sib_send,
    sib_recv,
    rs_send,
    rs_recv,
    ag_send,
    ag_recv,
):
    sec = lax.axis_index("pipe")
    me = lax.axis_index("dp")
    sections = lax.axis_size("pipe")
    ranks = lax.axis_size("dp")
    toks, width = x_hbm.shape
    units = u_v.shape[0]
    group_cols = width // ranks
    piece = units // ranks
    core = me % 2
    x_bit = (me // 2) % 2
    y_bit = me // 4
    sib = me + 1 - 2 * core
    nbr_x = me + 2 - 4 * x_bit
    nbr_y = me + 4 - 8 * y_bit
    diag = nbr_x + 4 - 8 * y_bit
    flip = 1 - 2 * core
    peers = (nbr_x, nbr_y, diag)

    def remote(src, dst, send, recv, pipe, dp):
        return pltpu.make_async_remote_copy(
            src_ref=src,
            dst_ref=dst,
            send_sem=send,
            recv_sem=recv,
            device_id=(pipe, dp),
            device_id_type=MESH,
        )

    def whole(src, dst, i):
        return [pltpu.make_async_copy(src, dst, in_sem.at[i, 0])]

    def grouped(src, dst, i):
        return [
            pltpu.make_async_copy(
                src.at[:, pl.ds(c * group_cols, group_cols)], dst.at[c], in_sem.at[i, c]
            )
            for c in range(ranks)
        ]

    loads = [
        whole(u_hbm, u_v, 0),
        grouped(x_hbm, x_v, 1),
        whole(v_hbm, v_v, 2),
        grouped(g_hbm, g_v, 3),
        grouped(m_hbm, m_v, 4),
        grouped(e_hbm, e_v, 5),
        whole(se_hbm, se_v, 6),
    ]
    for copies in loads:
        for load in copies:
            load.start()

    def loaded(i):
        for load in loads[i]:
            load.wait()

    barrier = pltpu.get_barrier_semaphore()
    for peer in (sib,) + peers:
        pl.semaphore_signal(barrier, inc=1, device_id=(sec, peer), device_id_type=MESH)
    for hop in range(1, sections):
        pl.semaphore_signal(
            barrier, inc=1, device_id=((sec + hop) % sections, me), device_id_type=MESH
        )
    pl.semaphore_wait(barrier, 3 + sections)

    def up_rows(j, rank, part=None):
        rows = pl.ds(pl.multiple_of(rank * piece, piece), piece)
        if part is None:
            return ups.at[j - 1, rows]
        start, size = ((0, width // 4), (width // 4, width // 4), (width // 2, width // 2))[part]
        return ups.at[j - 1, rows, pl.ds(start, size)]

    def z_own(j):
        rows = pl.ds(pl.multiple_of(me * piece, piece), piece)
        return remote(u_hbm.at[rows], up_rows(j, me), z_send.at[j - 1], z_recv.at[j - 1], j - 1, me)

    def z_pass(j):
        return remote(
            up_rows(j, me),
            up_rows(j, me),
            z_send.at[j - 1],
            z_recv.at[j - 1],
            jnp.maximum(sec - 1, 0),
            me,
        )

    def zd_own(j):
        src = u_hbm.at[
            pl.ds(pl.multiple_of(diag * piece, piece), piece), pl.ds(width // 2, width // 2)
        ]
        return remote(
            src, up_rows(j, diag, 2), zd_send.at[j - 1], zd_recv.at[j - 1], j - 1, me
        )

    def zd_pass(j):
        ref = up_rows(j, diag, 2)
        return remote(
            ref, ref, zd_send.at[j - 1], zd_recv.at[j - 1], jnp.maximum(sec - 1, 0), me
        )

    def zd_step(j):
        zd_pass(j).wait_recv()

        @pl.when(sec > 0)
        def _():
            zd_pass(j).start()

    for j in range(1, sections):

        @pl.when(sec == j)
        def _():
            z_own(j).start()

    def spread_copy(place, send, recv, i):
        ref, peer = (
            (place(me), nbr_x),
            (place(me), nbr_y),
            (place(nbr_x, 0), nbr_y),
            (place(nbr_y, 1), nbr_x),
            (place(me), sib),
            (place(nbr_x), sib),
            (place(nbr_y), sib),
            (place(diag), sib),
        )[i]
        return remote(ref, ref, send.at[i], recv.at[i], sec, peer)

    def arrive(place, send, recv, i):
        ref = (
            place(nbr_x),
            place(nbr_y),
            place(diag, 0),
            place(diag, 1),
            place(sib),
            place(nbr_x + flip),
            place(nbr_y + flip),
            place(diag + flip),
        )[i]
        remote(ref, ref, send.at[i], recv.at[i], sec, sib).wait_recv()

    def spread_start(*where):
        for i in (0, 1, 4):
            spread_copy(*where, i).start()

    def spread_pass(*where):
        for i in (0, 1):
            arrive(*where, i)
            spread_copy(*where, 2 + i).start()
            spread_copy(*where, 5 + i).start()

    def spread_diag(*where):
        arrive(*where, 2)
        arrive(*where, 3)
        spread_copy(*where, 7).start()

    def spread_finish(*where):
        for i in (4, 5, 6, 7):
            arrive(*where, i)

    def spread_drain(*where):
        for i in range(8):
            spread_copy(*where, i).wait_send()

    def up_args(j):
        return (functools.partial(up_rows, j), up_send.at[j - 1], up_recv.at[j - 1])

    contract = (((1,), (1,)), ((), ()))
    chunks = ranks

    def cols_of(i):
        return pl.ds(pl.multiple_of(i * group_cols, group_cols), group_cols)

    def contracted(left, right):
        total = jnp.zeros((toks, units), jnp.float32)
        for i in range(chunks):
            total = total + lax.dot_general(
                left(i),
                right[:, cols_of(i)],
                contract,
                preferred_element_type=jnp.float32,
            )
        return total

    def z_step(j):
        z_pass(j).wait_recv()

        @pl.when(sec > 0)
        def _():
            z_pass(j).start()

        spread_start(*up_args(j))

    above = sections - 1 - sec

    def turn(step, k):
        @pl.when(k <= above)
        def _():
            if step in (z_step, zd_step):
                step(sec + k)
            else:
                step(*up_args(sec + k))

    turn(z_step, 1)
    loaded(0)
    loaded(1)
    pre = contracted(lambda i: x_v[i], u_v)
    tanh = jnp.tanh(slope_c * (pre + slope_k * (pre * pre * pre)))
    act = 0.5 * pre * (1.0 + tanh)
    act_t[...] = jnp.transpose(act).astype(jnp.bfloat16)
    slope_v[...] = 0.5 * (1.0 + tanh) + (0.5 * slope_c) * pre * (1.0 - tanh * tanh) * (
        1.0 + 3.0 * slope_k * (pre * pre)
    )
    turn(z_step, 2)
    loaded(2)
    loaded(3)
    dact[...] = contracted(lambda i: g_v[i], v_v)
    turn(spread_pass, 1)
    turn(z_step, 3)
    for j in range(1, sections):

        @pl.when(sec == j)
        def _():
            zd_own(j).start()

    turn(spread_pass, 2)
    turn(zd_step, 1)
    turn(spread_diag, 1)
    turn(zd_step, 2)

    def cross(k):
        @pl.when(k <= above)
        def _():
            spread_finish(*up_args(sec + k))
            slot = sec + k - 1
            mixed[slot] = contracted(lambda i: ups[slot, :, cols_of(i)], v_v)

    turn(spread_pass, 3)
    turn(zd_step, 3)
    cross(1)
    turn(spread_diag, 2)
    turn(spread_diag, 3)
    cross(2)
    cross(3)

    for k in range(sections - 1, 0, -1):

        @pl.when(k <= above)
        def _():
            slot = sec + k - 1
            remote(
                pres.at[slot], pres.at[slot], pre_send.at[0], pre_recv.at[slot], sec, sib
            ).wait_recv()
            dact[...] += jnp.dot(
                pres[slot].astype(jnp.float32), mixed[slot], precision=lax.Precision.HIGHEST
            )

    d_pre = dact[...] * slope_v[...]
    pre_v[...] = d_pre.astype(jnp.bfloat16)
    pre_t[...] = jnp.transpose(d_pre).astype(jnp.bfloat16)

    def send_pre(target):
        slot = jnp.maximum(sec - 1, 0)
        return remote(pre_v, pres.at[slot], pre_send.at[target], pre_recv.at[slot], target, me)

    for target in range(sections - 2, -1, -1):

        @pl.when(target < sec)
        def _():
            send_pre(target).start()

    for low in range(sections - 1):

        @pl.when(sec == low)
        def _():
            @pl.loop(0, chunks)
            def _(i):
                wide = jnp.concatenate([pres[k] for k in range(low, sections - 1)], axis=1)
                tall = ups[low:, :, cols_of(i)].reshape((sections - 1 - low) * units, group_cols)
                step = jnp.dot(wide, tall, preferred_element_type=jnp.float32)
                g_v[i] = (g_v[i].astype(jnp.float32) + step).astype(jnp.bfloat16)

    for i in (4, 5, 6):
        loaded(i)

    rows = m_hbm.shape[0]
    entries = rows * group_cols
    steps = rows // row_step

    def rows_of(i):
        return pl.ds(pl.multiple_of(i * row_step, row_step), row_step)

    def magnitude(ref):
        def body(i, total):
            return total + jnp.abs(ref[rows_of(i)])

        total = lax.fori_loop(0, steps, body, jnp.zeros((row_step, group_cols), jnp.float32))
        return jnp.sum(total) / entries + epsilon

    def pack(rank, into):
        group = group_ref[rank]
        total = jnp.zeros((8, col_step), jnp.float32)
        for half, (weights, values) in enumerate(((pre_t, x_v), (act_t, g_v))):
            part = pl.ds(half * units, units)
            for k in range(group_cols // col_step):
                cols = pl.ds(k * col_step, col_step)
                value = (
                    0.9 * m_v[group, part, cols].astype(jnp.float32)
                    + 0.1
                    * jnp.dot(
                        weights[...], values[group, :, cols], preferred_element_type=jnp.float32
                    )
                    + e_v[group, part, cols].astype(jnp.float32)
                )
                comb[part, cols] = value
                total = total + jnp.sum(
                    jnp.abs(value).reshape(units // 8, 8, col_step), axis=0
                )
        scale = jnp.sum(total) / entries + epsilon
        inverse = 1.0 / scale

        @pl.loop(0, steps)
        def _(i):
            value = comb[rows_of(i)]
            packed = (scale * jnp.tanh(value * inverse)).astype(jnp.bfloat16)
            into[rows_of(i)] = packed
            work_v[rank, rows_of(i)] = (value - packed.astype(jnp.float32)).astype(jnp.bfloat16)

        pltpu.make_async_copy(work_v.at[rank], work_out.at[rank], out_sem.at[rank]).start()

    dests = (diag, nbr_x, nbr_y, me)

    def sib_copy(i):
        return remote(sib_out.at[i], sib_in.at[i], sib_send.at[i], sib_recv.at[i], sec, sib)

    half_rows = rows // 2

    def rs_copy(i):
        part = pl.ds((i % 2) * half_rows, half_rows)
        peer = (nbr_x, nbr_y, nbr_x, nbr_x, nbr_y, nbr_y)[i]
        return remote(
            rs_out.at[i // 2, part],
            rs_in.at[i // 2, part],
            rs_send.at[i],
            rs_recv.at[i],
            sec,
            peer,
        )

    def carry(arrived, slot):
        rs_copy(arrived).wait_recv()
        first = (arrived % 2) * (half_rows // row_step)

        @pl.loop(first, first + half_rows // row_step)
        def _(k):
            rs_out[slot, rows_of(k)] = (
                rs_out[slot, rows_of(k)].astype(jnp.float32)
                + rs_in[0, rows_of(k)].astype(jnp.float32)
            ).astype(jnp.bfloat16)

    for i, dest in enumerate(dests):
        pack(dest + flip, sib_out.at[i])
        sib_copy(i).start()
        pack(dest, own_pack)
        sib_copy(i).wait_recv()

        @pl.loop(0, steps)
        def _(k):
            both = own_pack[rows_of(k)].astype(jnp.float32) + sib_in[i, rows_of(k)].astype(
                jnp.float32
            )
            if i < 3:
                rs_out[i, rows_of(k)] = both.astype(jnp.bfloat16)
            else:
                own_sum[rows_of(k)] = both

        if i == 0:
            rs_copy(0).start()
            rs_copy(1).start()
        if i == 1:
            rs_copy(2).start()
        if i == 2:
            rs_copy(5).start()
            carry(1, 1)
            rs_copy(3).start()
            carry(0, 2)
            rs_copy(4).start()

    for i in range(2, 6):
        rs_copy(i).wait_recv()

    @pl.loop(0, steps)
    def _(k):
        total = own_sum[rows_of(k)]
        for i in (1, 2):
            total = total + rs_in[i, rows_of(k)].astype(jnp.float32)
        comb[rows_of(k)] = total * (1.0 / ranks) + se_v[rows_of(k)]

    scale = magnitude(comb)
    inverse = 1.0 / scale

    @pl.loop(0, steps)
    def _(k):
        value = comb[rows_of(k)]
        packed = (scale * jnp.tanh(value * inverse)).astype(jnp.bfloat16)
        gath[me, rows_of(k)] = packed
        own_sum[rows_of(k)] = value - packed.astype(jnp.float32)

    def gath_place(t, rank, part=None):
        size = rows // ag_chunks
        if part is None:
            return gath.at[rank, pl.ds(t * size, size)]
        return gath.at[rank, pl.ds(t * size + part * (size // 2), size // 2)]

    def ag_args(t):
        return (functools.partial(gath_place, t), ag_send.at[t], ag_recv.at[t])

    for t in range(ag_chunks):
        spread_start(*ag_args(t))

    def keep(i, rank):
        return pltpu.make_async_copy(gath.at[rank], mom_out.at[rank], in_sem.at[1, i])

    kept = (me, nbr_x, nbr_y, diag, sib, nbr_x + flip, nbr_y + flip, diag + flip)
    keep(0, me).start()
    serv_copy = pltpu.make_async_copy(own_sum, serv_out, in_sem.at[0, 0])
    serv_copy.start()

    for rank in range(ranks):
        pltpu.make_async_copy(work_v.at[rank], work_out.at[rank], out_sem.at[rank]).wait()
    for t in range(ag_chunks + 1):
        if t < ag_chunks:
            spread_pass(*ag_args(t))
        if t > 0:
            spread_diag(*ag_args(t - 1))
    for i in (1, 2, 3):
        keep(i, kept[i]).start()
    serv_copy.wait()
    for i in (4, 5, 6, 7):
        for t in range(ag_chunks):
            arrive(*ag_args(t), i)
        keep(i, kept[i]).start()
    for t in range(ag_chunks):
        spread_drain(*ag_args(t))
    for i in range(4):
        sib_copy(i).wait_send()
    for i in range(6):
        rs_copy(i).wait_send()
    for target in range(sections - 1):

        @pl.when(target < sec)
        def _():
            send_pre(target).wait_send()

    for j in range(1, sections):

        @pl.when(sec == j)
        def _():
            z_own(j).wait_send()
            zd_own(j).wait_send()

        @pl.when(j > sec)
        def _():
            spread_drain(*up_args(j))

            @pl.when(sec > 0)
            def _():
                z_pass(j).wait_send()
                zd_pass(j).wait_send()

    for i in range(8):
        keep(i, kept[i]).wait()


def place_kernel(
    owner_ref, mom_ref, work_ref, serv_ref, mom_out, work_out, serv_out, held, kept, load_sem, store_sem
):
    ranks, rows, cols = mom_ref.shape
    loads = [pltpu.make_async_copy(serv_ref, kept, load_sem.at[2, 0])]
    stores = [pltpu.make_async_copy(kept, serv_out, store_sem.at[2, 0])]
    for i, (src, dst) in enumerate(((work_ref, work_out), (mom_ref, mom_out))):
        for c in range(ranks):
            loads.append(
                pltpu.make_async_copy(src.at[owner_ref[c]], held.at[i, c], load_sem.at[i, c])
            )
            stores.append(
                pltpu.make_async_copy(
                    held.at[i, c], dst.at[:, pl.ds(c * cols, cols)], store_sem.at[i, c]
                )
            )
    for load in loads:
        load.start()
    for load, store in zip(loads, stores):
        load.wait()
        store.start()
    for store in stores:
        store.wait()


def fused_on_device(
    section_inputs,
    out_grad,
    up_weight,
    down_weight,
    momentum,
    worker_error,
    server_error,
    owner_map,
):
    sections = lax.axis_size("pipe")
    ranks = lax.axis_size("dp")
    toks, width = section_inputs.shape
    units = up_weight.shape[0]
    rows = momentum.shape[0]
    group_cols = width // ranks
    bf16, f32 = jnp.bfloat16, jnp.float32
    dma = pltpu.SemaphoreType.DMA
    hbm = pl.BlockSpec(memory_space=pl.ANY)
    block = (rows, group_cols)
    order = jnp.arange(ranks, dtype=jnp.int32)
    rank_group = jnp.sum(jnp.where(owner_map[None, :] == order[:, None], order[None, :], 0), axis=1)
    moms, works, serv = pl.pallas_call(
        fused_kernel,
        out_shape=(
            jax.ShapeDtypeStruct((ranks,) + block, bf16),
            jax.ShapeDtypeStruct((ranks,) + block, bf16),
            jax.ShapeDtypeStruct(block, f32),
        ),
        in_specs=[pl.BlockSpec(memory_space=pltpu.SMEM)] + [hbm] * 7,
        out_specs=(hbm, hbm, hbm),
        scratch_shapes=[
            pltpu.VMEM((ranks, toks, group_cols), bf16),
            pltpu.VMEM((ranks, toks, group_cols), bf16),
            pltpu.VMEM((units, width), bf16),
            pltpu.VMEM((units, width), bf16),
            pltpu.VMEM((ranks,) + block, bf16),
            pltpu.VMEM((ranks,) + block, bf16),
            pltpu.VMEM(block, f32),
            pltpu.VMEM((sections - 1, units, width), bf16),
            pltpu.VMEM((sections - 1, toks, units), bf16),
            pltpu.VMEM((units, toks), bf16),
            pltpu.VMEM((toks, units), f32),
            pltpu.VMEM((toks, units), bf16),
            pltpu.VMEM((units, toks), bf16),
            pltpu.VMEM((toks, units), f32),
            pltpu.VMEM((sections - 1, units, units), f32),
            pltpu.VMEM(block, f32),
            pltpu.VMEM(block, bf16),
            pltpu.VMEM(block, f32),
            pltpu.VMEM((ranks,) + block, bf16),
            pltpu.VMEM((4,) + block, bf16),
            pltpu.VMEM((4,) + block, bf16),
            pltpu.VMEM((3,) + block, bf16),
            pltpu.VMEM((3,) + block, bf16),
            pltpu.VMEM((ranks,) + block, bf16),
            dma((7, ranks)),
            dma((ranks,)),
            dma((sections - 1,)),
            dma((sections - 1,)),
            dma((sections - 1,)),
            dma((sections - 1,)),
            dma((sections - 1, 8)),
            dma((sections - 1, 8)),
            dma((sections - 1,)),
            dma((sections - 1,)),
            dma((4,)),
            dma((4,)),
            dma((6,)),
            dma((6,)),
            dma((ag_chunks, 8)),
            dma((ag_chunks, 8)),
        ],
        compiler_params=pltpu.CompilerParams(
            collective_id=0, has_side_effects=True, vmem_limit_bytes=56 * 1024 * 1024
        ),
        name="adapter_step",
    )(
        rank_group,
        section_inputs,
        out_grad,
        up_weight,
        down_weight,
        momentum,
        worker_error,
        server_error,
    )
    return pl.pallas_call(
        place_kernel,
        out_shape=(
            jax.ShapeDtypeStruct((rows, width), bf16),
            jax.ShapeDtypeStruct((rows, width), bf16),
            jax.ShapeDtypeStruct(block, f32),
        ),
        in_specs=[pl.BlockSpec(memory_space=pltpu.SMEM), hbm, hbm, hbm],
        out_specs=(hbm, hbm, hbm),
        scratch_shapes=[
            pltpu.VMEM((2, ranks) + block, bf16),
            pltpu.VMEM(block, f32),
            dma((3, ranks)),
            dma((3, ranks)),
        ],
        compiler_params=pltpu.CompilerParams(vmem_limit_bytes=60 * 1024 * 1024),
        name="place_groups",
    )(owner_map, moms, works, serv)


def solution(mesh):
    in_specs = (
        P(("pipe", "dp"), None),
        P("dp", None),
        P("pipe", None),
        P("pipe", None),
        P("pipe", None),
        P("pipe", "dp"),
        P("pipe", "dp"),
        P(),
    )
    out_specs = (P("pipe", None), P("pipe", "dp"), P("pipe", "dp"))
    fits = mesh.shape["dp"] == 8 and mesh.shape["pipe"] == 4
    return jax.shard_map(
        fused_on_device if fits else on_device, mesh=mesh, in_specs=in_specs, out_specs=out_specs, check_vma=False
    )
```
